32 devices in a mesh: section: 4 (over z), row: 4 (over x, core), col: 2 (over y).
Axes of the slice: x: 2, y: 2, z: 4, core: 2. Of those that a mesh axis runs over, the one named last changes fastest.
Arguments:
- state: bfloat16 [4, 128, 64, 256], P('section', 'row', 'col'), may hold values from -6 to 6
- fresh: bfloat16 [128, 64, 256], P('row', 'col'), may hold values from -6 to 6
- conv_first: bfloat16 [4, 3, 3, 256, 256], P('section'), may hold values from -0.125 to 0.125
- conv_second: bfloat16 [4, 3, 3, 256, 256], P('section'), may hold values from -0.125 to 0.125
- gains: float32 [4, 2, 256], P('section'), may hold values from 0.1 to 1.9
- shifts: float32 [4, 2, 256], P('section'), may hold values from -2.4 to 2.4
Outputs:
- blocks: bfloat16 [2, 4, 128, 64, 256], P(None, 'section', 'row', 'col')
The draws below stay inside these ranges and needn't reach their ends.
All inputs are finite; a program needn't handle non-finite values.
Results may differ from the reference program's by a relative error of at most 0.005.
Values may be sent and summed in bfloat16 or wider, within the bound.
A program may use at most 64 MiB of HBM per device.

```python
import jax
import jax.numpy as jnp
from jax import lax

C = 256
TICKS = 2
SECTIONS = 4
NH = 128
NW = 64


def shard_levels(rng, extent, split, smallest, high):
    loudness, own = 1.0, jax.random.fold_in(rng, 6)
    for axis_at, parts in split:
        draws = jnp.exp(jax.random.uniform(jax.random.fold_in(own, axis_at), (parts,), jnp.float32, smallest / len(split), high / len(split)))
        loudness = loudness * jnp.repeat(draws, extent[axis_at] // parts).reshape([-1 if axis == axis_at else 1 for axis in range(len(extent))])
    return loudness


def gaussian(rng, dims, scale, reach, split=(), held_as=jnp.bfloat16):
    values = jax.random.normal(rng, dims, jnp.float32) * scale
    if len(split) > 0:
        values = shard_levels(rng, dims, split, -0.22, 0.18) * values
    return jnp.clip(values, min=-reach, max=reach).astype(held_as)


def setup_inputs(seed: int = 0) -> dict:
    key_of = jax.random.split(jax.random.key(seed), 7)
    return {
        "state": gaussian(key_of[0], (SECTIONS, NH, NW, C), 1.0, 6.0, ((0, 4), (1, 4), (2, 2))),
        "fresh": gaussian(key_of[1], (NH, NW, C), 1.0, 6.0, ((0, 4), (1, 2))),
        "conv_first": gaussian(key_of[2], (SECTIONS, 3, 3, C, C), (9 * C) ** -0.5, 0.125, ((0, 4),)),
        "conv_second": gaussian(key_of[3], (SECTIONS, 3, 3, C, C), (9 * C) ** -0.5, 0.125, ((0, 4),)),
        "gains": jnp.clip(1.0 + 0.18 * jax.random.normal(key_of[4], (SECTIONS, 2, C), jnp.float32), 0.1, 1.9),
        "shifts": gaussian(key_of[5], (SECTIONS, 2, C), 0.4, 2.4, ((0, 4),), jnp.float32),
    }


def convolve(features, kernel):
    result = lax.conv_general_dilated(features.astype(jnp.float32)[None], kernel.astype(jnp.float32), (1, 1), "SAME", dimension_numbers=("NHWC", "HWIO", "NHWC"), precision=lax.Precision.HIGHEST)
    return result[0]


def section_block(features, first_kernel, second_kernel, gain_pair, shift_pair):
    hidden = jax.nn.relu(gain_pair[0] * convolve(features, first_kernel) + shift_pair[0]).astype(jnp.bfloat16)
    summed = features.astype(jnp.float32) + gain_pair[1] * convolve(hidden, second_kernel) + shift_pair[1]
    return jax.nn.relu(summed).astype(jnp.bfloat16)


def reference(state, fresh, conv_first, conv_second, gains, shifts):
    current = [state[section_index] for section_index in range(SECTIONS)]
    per_tick = []
    for tick_index in range(TICKS):
        outputs = [section_block(current[section_index], conv_first[section_index], conv_second[section_index], gains[section_index], shifts[section_index]) for section_index in range(SECTIONS)]
        per_tick.append(jnp.stack(outputs))
        current = [fresh] + outputs[:-1]
    return jnp.stack(per_tick)
```

```python
import functools

import jax
import jax.numpy as jnp
from jax import lax
from jax.experimental import pallas as pl
from jax.experimental.pallas import tpu as pltpu
from jax.sharding import PartitionSpec as P

TICKS = 2
CHUNK = 8
DIRECTIONS = ((-1, 0), (1, 0), (0, -1), (0, 1), (-1, -1), (-1, 1), (1, -1), (1, 1))
MESH = pl.DeviceIdType.MESH


def kernel(
    sections, rows_n, cols_n,
    state, fresh, first, second, gains, shifts, out,
    x0, x1, out0, out1, w1, w2, stk_x, stk_h,
    out_row, out_col, halo_row, halo_col, halo_cor,
    in_sem, out_sem, send_sem, recv_sem, sec_send, sec_recv,
):
    height, width, chan = x0.shape
    chunks = height // CHUNK
    sec = lax.axis_index("section")
    row = lax.axis_index("row")
    col = lax.axis_index("col")

    def exists(dr, dc):
        return (row + dr >= 0) & (row + dr < rows_n) & (col + dc >= 0) & (col + dc < cols_n)

    def target(dr, dc):
        return {"row": row + dr, "col": col + dc}

    ins = [
        pltpu.make_async_copy(state, x0, in_sem.at[0]),
        pltpu.make_async_copy(first, w1, in_sem.at[1]),
        pltpu.make_async_copy(second, w2, in_sem.at[2]),
    ]
    fresh_copy = pltpu.make_async_copy(fresh, x1, in_sem.at[3])
    for copy in ins:
        copy.start()

    @pl.when(sec == 0)
    def _():
        fresh_copy.start()

    halo_row[...] = jnp.zeros_like(halo_row)
    halo_col[...] = jnp.zeros_like(halo_col)
    halo_cor[...] = jnp.zeros_like(halo_cor)

    barrier = pltpu.get_barrier_semaphore()
    count = jnp.int32(0)
    for dr, dc in DIRECTIONS:
        there = exists(dr, dc)
        count = count + there.astype(jnp.int32)

        @pl.when(there)
        def _(dr=dr, dc=dc):
            pl.semaphore_signal(barrier, inc=1, device_id=target(dr, dc), device_id_type=MESH)

    for ds in (-1, 1):
        there = (sec + ds >= 0) & (sec + ds < sections)
        count = count + there.astype(jnp.int32)

        @pl.when(there)
        def _(ds=ds):
            pl.semaphore_signal(barrier, inc=1, device_id={"section": sec + ds}, device_id_type=MESH)

    pl.semaphore_wait(barrier, count)

    def edge_copy(e, d):
        dr, dc = DIRECTIONS[d]
        if dc == 0:
            src, dst = out_row.at[e, (dr + 1) // 2], halo_row.at[e, (1 - dr) // 2]
        elif dr == 0:
            src, dst = out_col.at[e, (dc + 1) // 2], halo_col.at[e, (1 - dc) // 2]
        else:
            start = 0 if dr < 0 else height - 8
            src = out_col.at[e, (dc + 1) // 2, pl.ds(start, 8)]
            dst = halo_cor.at[e, (1 - dr) // 2, (1 - dc) // 2]
        return pltpu.make_async_remote_copy(
            src_ref=src, dst_ref=dst, send_sem=send_sem.at[e, d], recv_sem=recv_sem.at[e, d],
            device_id=target(dr, dc), device_id_type=MESH,
        )

    def send_edges(e, which):
        for d in which:
            @pl.when(exists(*DIRECTIONS[d]))
            def _(d=d):
                edge_copy(e, d).start()

    def receive_edges(e):
        for d, (dr, dc) in enumerate(DIRECTIONS):
            @pl.when(exists(-dr, -dc))
            def _(d=d):
                edge_copy(e, d).wait_recv()

    def column(shape):
        return lax.broadcasted_iota(jnp.int32, shape, 1)

    def put(stk, at, values, left, right):
        n = values.shape[0]
        at_col = column(values.shape)
        stk[pl.ds(at, n), :, chan : 2 * chan] = values.astype(jnp.bfloat16)
        stk[pl.ds(at, n), :, :chan] = jnp.where(
            at_col == 0, left, pltpu.roll(values, 1, 1)).astype(jnp.bfloat16)
        stk[pl.ds(at, n), :, 2 * chan :] = jnp.where(
            at_col == width - 1, right, pltpu.roll(values, width - 1, 1)).astype(jnp.bfloat16)

    def put_main(e, stk, start, values):
        put(stk, start + 1, values, 0.0, 0.0)
        rows = pl.ds(pl.multiple_of(start, CHUNK), CHUNK)
        out_col[e, 0, rows] = values[:, 0, :]
        out_col[e, 1, rows] = values[:, width - 1, :]

    def finish(e, stk):
        receive_edges(e)
        for side in range(2):
            at = 0 if side == 0 else height + 1
            line = 7 if side == 0 else 0
            put(
                stk, at, halo_row[e, side].astype(jnp.float32)[None],
                halo_cor[e, side, 0][line : line + 1][None],
                halo_cor[e, side, 1][line : line + 1][None],
            )

        @pl.loop(0, chunks)
        def _(k):
            start = pl.multiple_of(k * CHUNK, CHUNK)
            for side in range(2):
                part = pl.ds(0, 16) if side == 0 else pl.ds(width - 16, 16)
                lanes = pl.ds(2 * chan * side, chan)
                old = stk[pl.ds(start + 1, CHUNK), part, lanes].astype(jnp.float32)
                edge = halo_col[e, side, pl.ds(start, CHUNK)].reshape(CHUNK, 1, chan)
                stk[pl.ds(start + 1, CHUNK), part, lanes] = jnp.where(
                    column(old.shape) == 15 * side, edge, old).astype(jnp.bfloat16)

    def conv(stk, w, start):
        total = None
        for tap in range(3):
            part = stk[pl.ds(start + tap, CHUNK)].reshape(CHUNK * width, 3 * chan)
            dot = jnp.dot(part, w[tap], preferred_element_type=jnp.float32)
            total = dot if total is None else total + dot
        return total

    def section_copy(k):
        rows = pl.ds(k * CHUNK, CHUNK)
        return pltpu.make_async_remote_copy(
            src_ref=out0.at[rows], dst_ref=x1.at[rows],
            send_sem=sec_send.at[k], recv_sem=sec_recv.at[k],
            device_id={"section": sec + 1}, device_id_type=MESH,
        )

    def result_copy(tick, k):
        rows = pl.ds(k * CHUNK, CHUNK)
        src = out0 if tick == 0 else out1
        return pltpu.make_async_copy(src.at[rows], out.at[tick, rows], out_sem.at[tick, k])

    for tick in range(TICKS):
        x = x0 if tick == 0 else x1
        e = 2 * tick
        if tick == 0:
            ins[0].wait()
        else:
            @pl.when(sec == 0)
            def _():
                fresh_copy.wait()

        @pl.loop(0, chunks)
        def _(k):
            if tick > 0:
                @pl.when(sec > 0)
                def _():
                    section_copy(k).wait_recv()
            put_main(e, stk_x, k * CHUNK, x[pl.ds(k * CHUNK, CHUNK)].astype(jnp.float32))

        out_row[e, 0] = x[0]
        out_row[e, 1] = x[height - 1]
        send_edges(e, range(8))
        if tick == 0:
            ins[1].wait()
        finish(e, stk_x)

        @pl.loop(0, chunks)
        def _(k):
            total = conv(stk_x, w1, k * CHUNK)
            hidden = jnp.maximum(gains[0:1] * total + shifts[0:1], 0.0)
            hidden = hidden.astype(jnp.bfloat16).astype(jnp.float32)
            put_main(e + 1, stk_h, k * CHUNK, hidden.reshape(CHUNK, width, chan))

        out_row[e + 1, 0] = stk_h[1, :, chan : 2 * chan]
        out_row[e + 1, 1] = stk_h[height, :, chan : 2 * chan]
        send_edges(e + 1, range(8))
        if tick == 0:
            ins[2].wait()
        finish(e + 1, stk_h)

        @pl.loop(0, chunks)
        def _(k):
            total = gains[1:2] * conv(stk_h, w2, k * CHUNK) + shifts[1:2]
            rows = pl.ds(k * CHUNK, CHUNK)
            summed = x[rows].astype(jnp.float32) + total.reshape(CHUNK, width, chan)
            result = out0 if tick == 0 else out1
            result[rows] = jnp.maximum(summed, 0.0).astype(jnp.bfloat16)
            if tick == 0:
                @pl.when(sec + 1 < sections)
                def _():
                    section_copy(k).start()
            result_copy(tick, k).start()

    for tick in range(TICKS):
        @pl.loop(0, chunks)
        def _(k):
            result_copy(tick, k).wait()

    @pl.when(sec + 1 < sections)
    def _():
        @pl.loop(0, chunks)
        def _(k):
            section_copy(k).wait_send()

    for e in range(2 * TICKS):
        for d, (dr, dc) in enumerate(DIRECTIONS):
            @pl.when(exists(dr, dc))
            def _(e=e, d=d):
                edge_copy(e, d).wait_send()


def per_device(sizes, state, fresh, conv_first, conv_second, gains, shifts):
    height, width, chan = fresh.shape
    chunks = height // CHUNK
    first = conv_first[0].reshape(3, 3 * chan, chan)
    second = conv_second[0].reshape(3, 3 * chan, chan)
    steps = 2 * TICKS
    tile = pltpu.VMEM((height, width, chan), jnp.bfloat16)
    weight = pltpu.VMEM((3, 3 * chan, chan), jnp.bfloat16)
    stack = pltpu.VMEM((height + 2, width, 3 * chan), jnp.bfloat16)
    anywhere = pl.BlockSpec(memory_space=pl.ANY)
    in_vmem = pl.BlockSpec(memory_space=pltpu.VMEM)
    result = pl.pallas_call(
        functools.partial(kernel, *sizes),
        out_shape=jax.ShapeDtypeStruct((TICKS, height, width, chan), jnp.bfloat16),
        in_specs=[anywhere] * 4 + [in_vmem] * 2,
        out_specs=anywhere,
        scratch_shapes=[
            tile, tile, tile, tile, weight, weight, stack, stack,
            pltpu.VMEM((steps, 2, width, chan), jnp.bfloat16),
            pltpu.VMEM((steps, 2, height, chan), jnp.float32),
            pltpu.VMEM((steps, 2, width, chan), jnp.bfloat16),
            pltpu.VMEM((steps, 2, height, chan), jnp.float32),
            pltpu.VMEM((steps, 2, 2, 8, chan), jnp.float32),
            pltpu.SemaphoreType.DMA((4,)),
            pltpu.SemaphoreType.DMA((TICKS, chunks)),
            pltpu.SemaphoreType.DMA((steps, 8)),
            pltpu.SemaphoreType.DMA((steps, 8)),
            pltpu.SemaphoreType.DMA((chunks,)),
            pltpu.SemaphoreType.DMA((chunks,)),
        ],
        compiler_params=pltpu.CompilerParams(
            collective_id=0, has_side_effects=True, vmem_limit_bytes=40 * 1024 * 1024
        ),
    )(state[0], fresh, first, second, gains[0], shifts[0])
    return result[:, None]


def solution(mesh):
    sizes = tuple(mesh.shape[axis] for axis in ("section", "row", "col"))
    in_specs = (
        P("section", "row", "col", None),
        P("row", "col", None),
        P("section", None, None, None, None),
        P("section", None, None, None, None),
        P("section", None, None),
        P("section", None, None),
    )
    out_specs = P(None, "section", "row", "col", None)
    return jax.shard_map(
        functools.partial(per_device, sizes),
        mesh=mesh, in_specs=in_specs, out_specs=out_specs, check_vma=False,
    )
```

```python
import functools

import jax
import jax.numpy as jnp
from jax import lax
from jax.experimental import pallas as pl
from jax.experimental.pallas import tpu as pltpu
from jax.sharding import PartitionSpec as P

TICKS = 2
CHUNK = 8
DIRECTIONS = ((-1, 0), (1, 0), (0, -1), (0, 1), (-1, -1), (-1, 1), (1, -1), (1, 1))
MESH = pl.DeviceIdType.MESH


def kernel(
    sections, rows_n, cols_n,
    state, fresh, first, second, gains_in, shifts_in, out,
    gains, shifts, x0, x1, out0, out1, w1, w2, stk_x, stk_h,
    out_row, out_col, halo_row, halo_col, halo_cor,
    in_sem, out_sem, send_sem, recv_sem, col_send, col_recv, sec_send, sec_recv,
):
    height, width, chan = x0.shape
    chunks = height // CHUNK
    sec = lax.axis_index("section")
    row = lax.axis_index("row")
    col = lax.axis_index("col")

    def exists(dr, dc):
        return (row + dr >= 0) & (row + dr < rows_n) & (col + dc >= 0) & (col + dc < cols_n)

    def target(dr, dc):
        return {"row": row + dr, "col": col + dc}

    copies = [
        pltpu.make_async_copy(src, dst, in_sem.at[n])
        for n, (src, dst) in enumerate(
            ((state, x0), (first, w1), (gains_in, gains), (shifts_in, shifts), (second, w2))
        )
    ]
    fresh_copy = pltpu.make_async_copy(fresh, x1, in_sem.at[5])
    for copy in copies:
        copy.start()

    @pl.when(sec == 0)
    def _():
        fresh_copy.start()

    halo_row[...] = jnp.zeros_like(halo_row)
    halo_col[...] = jnp.zeros_like(halo_col)
    halo_cor[...] = jnp.zeros_like(halo_cor)

    barrier = pltpu.get_barrier_semaphore()
    count = jnp.int32(0)
    for dr, dc in DIRECTIONS:
        there = exists(dr, dc)
        count = count + there.astype(jnp.int32)

        @pl.when(there)
        def _(dr=dr, dc=dc):
            pl.semaphore_signal(barrier, inc=1, device_id=target(dr, dc), device_id_type=MESH)

    for ds in (-1, 1):
        there = (sec + ds >= 0) & (sec + ds < sections)
        count = count + there.astype(jnp.int32)

        @pl.when(there)
        def _(ds=ds):
            pl.semaphore_signal(barrier, inc=1, device_id={"section": sec + ds}, device_id_type=MESH)

    def edge_copy(e, d):
        dr, dc = DIRECTIONS[d]
        if dc == 0:
            src, dst = out_row.at[e, (dr + 1) // 2], halo_row.at[e, (1 - dr) // 2]
        else:
            start = 0 if dr < 0 else height - 8
            src = out_col.at[e, (dc + 1) // 2, pl.ds(start, 8)]
            dst = halo_cor.at[e, (1 - dr) // 2, (1 - dc) // 2]
        return pltpu.make_async_remote_copy(
            src_ref=src, dst_ref=dst, send_sem=send_sem.at[e, d], recv_sem=recv_sem.at[e, d],
            device_id=target(dr, dc), device_id_type=MESH,
        )

    def col_copy(e, side, k):
        rows = pl.ds(pl.multiple_of(k * CHUNK, CHUNK), CHUNK)
        return pltpu.make_async_remote_copy(
            src_ref=out_col.at[e, side, rows], dst_ref=halo_col.at[e, 1 - side, rows],
            send_sem=col_send.at[e, side, k], recv_sem=col_recv.at[e, side, k],
            device_id=target(0, 2 * side - 1), device_id_type=MESH,
        )

    def send_rows(e, way):
        for d, (dr, dc) in enumerate(DIRECTIONS):
            if dr == way:
                @pl.when(exists(dr, dc))
                def _(d=d):
                    edge_copy(e, d).start()

    def send(e, k):
        for side in range(2):
            @pl.when(exists(0, 2 * side - 1))
            def _(side=side):
                col_copy(e, side, k).start()

        @pl.when(k == 0)
        def _():
            send_rows(e, -1)

        @pl.when(k == chunks - 1)
        def _():
            send_rows(e, 1)

    def column(shape):
        return lax.broadcasted_iota(jnp.int32, shape, 1)

    def put(stk, at, values, left, right):
        n = values.shape[0]
        at_col = column(values.shape)
        stk[pl.ds(at, n), :, chan : 2 * chan] = values.astype(jnp.bfloat16)
        stk[pl.ds(at, n), :, :chan] = jnp.where(
            at_col == 0, left, pltpu.roll(values, 1, 1)).astype(jnp.bfloat16)
        stk[pl.ds(at, n), :, 2 * chan :] = jnp.where(
            at_col == width - 1, right, pltpu.roll(values, width - 1, 1)).astype(jnp.bfloat16)

    def put_main(e, stk, start, values):
        put(stk, start + 1, values, 0.0, 0.0)
        rows = pl.ds(pl.multiple_of(start, CHUNK), CHUNK)
        out_col[e, 0, rows] = values[:, 0, :]
        out_col[e, 1, rows] = values[:, width - 1, :]

    def fix_row(e, stk, side):
        for d, (dr, dc) in enumerate(DIRECTIONS):
            if dr == 1 - 2 * side:
                @pl.when(exists(-dr, -dc))
                def _(d=d):
                    edge_copy(e, d).wait_recv()
        at = 0 if side == 0 else height + 1
        line = 7 if side == 0 else 0
        put(
            stk, at, halo_row[e, side].astype(jnp.float32)[None],
            halo_cor[e, side, 0][line : line + 1][None],
            halo_cor[e, side, 1][line : line + 1][None],
        )

    def fix(e, stk, k):
        start = pl.multiple_of(k * CHUNK, CHUNK)
        for side in range(2):
            @pl.when(exists(0, 2 * side - 1))
            def _(side=side):
                col_copy(e, 1 - side, k).wait_recv()
                part = pl.ds(0, 16) if side == 0 else pl.ds(width - 16, 16)
                lanes = pl.ds(2 * chan * side, chan)
                old = stk[pl.ds(start + 1, CHUNK), part, lanes].astype(jnp.float32)
                edge = halo_col[e, side, pl.ds(start, CHUNK)].reshape(CHUNK, 1, chan)
                stk[pl.ds(start + 1, CHUNK), part, lanes] = jnp.where(
                    column(old.shape) == 15 * side, edge, old).astype(jnp.bfloat16)

        @pl.when(k == 0)
        def _():
            fix_row(e, stk, 0)

        @pl.when(k == chunks - 1)
        def _():
            fix_row(e, stk, 1)

    def conv(stk, w, start):
        total = None
        for tap in range(3):
            part = stk[pl.ds(start + tap, CHUNK)].reshape(CHUNK * width, 3 * chan)
            dot = jnp.dot(part, w[tap], preferred_element_type=jnp.float32)
            total = dot if total is None else total + dot
        return total

    def section_copy(k):
        rows = pl.ds(k * CHUNK, CHUNK)
        return pltpu.make_async_remote_copy(
            src_ref=out0.at[rows], dst_ref=x1.at[rows],
            send_sem=sec_send.at[k], recv_sem=sec_recv.at[k],
            device_id={"section": sec + 1}, device_id_type=MESH,
        )

    def result_copy(tick, k):
        rows = pl.ds(k * CHUNK, CHUNK)
        src = out0 if tick == 0 else out1
        return pltpu.make_async_copy(src.at[rows], out.at[tick, rows], out_sem.at[tick, k])

    def load(tick, k):
        x = x0 if tick == 0 else x1
        e = 2 * tick
        put_main(e, stk_x, k * CHUNK, x[pl.ds(k * CHUNK, CHUNK)].astype(jnp.float32))

        @pl.when(k == 0)
        def _():
            out_row[e, 0] = x[0]

        @pl.when(k == chunks - 1)
        def _():
            out_row[e, 1] = x[height - 1]

    def first_conv(tick, k):
        e = 2 * tick + 1
        total = conv(stk_x, w1, k * CHUNK)
        hidden = jnp.maximum(gains[0:1] * total + shifts[0:1], 0.0)
        hidden = hidden.astype(jnp.bfloat16).astype(jnp.float32)
        put_main(e, stk_h, k * CHUNK, hidden.reshape(CHUNK, width, chan))

        @pl.when(k == 0)
        def _():
            out_row[e, 0] = stk_h[1, :, chan : 2 * chan]

        @pl.when(k == chunks - 1)
        def _():
            out_row[e, 1] = stk_h[height, :, chan : 2 * chan]

        send(e, k)

    def second_conv(tick, k):
        x = x0 if tick == 0 else x1
        total = gains[1:2] * conv(stk_h, w2, k * CHUNK) + shifts[1:2]
        rows = pl.ds(k * CHUNK, CHUNK)
        summed = x[rows].astype(jnp.float32) + total.reshape(CHUNK, width, chan)
        result = out0 if tick == 0 else out1
        result[rows] = jnp.maximum(summed, 0.0).astype(jnp.bfloat16)
        if tick == 0:
            @pl.when(sec + 1 < sections)
            def _():
                section_copy(k).start()
        result_copy(tick, k).start()

    copies[0].wait()

    @pl.loop(0, chunks)
    def _(k):
        load(0, k)

    pl.semaphore_wait(barrier, count)

    @pl.loop(0, chunks)
    def _(k):
        send(0, k)

    for copy in copies[1:]:
        copy.wait()

    for tick in range(TICKS):
        if tick > 0:
            @pl.when(sec == 0)
            def _():
                fresh_copy.wait()

        @pl.loop(0 if tick else 1, chunks + 4)
        def _(i, tick=tick):
            if tick > 0:
                @pl.when(i < chunks)
                def _():
                    @pl.when(sec > 0)
                    def _():
                        section_copy(i).wait_recv()
                    load(tick, i)
                    send(2 * tick, i)

            @pl.when((i >= 1) & (i < chunks + 1))
            def _():
                fix(2 * tick, stk_x, i - 1)

            @pl.when((i >= 2) & (i < chunks + 2))
            def _():
                first_conv(tick, i - 2)

            @pl.when((i >= 3) & (i < chunks + 3))
            def _():
                fix(2 * tick + 1, stk_h, i - 3)

            @pl.when(i >= 4)
            def _():
                second_conv(tick, i - 4)

    for tick in range(TICKS):
        @pl.loop(0, chunks)
        def _(k):
            result_copy(tick, k).wait()

    @pl.when(sec + 1 < sections)
    def _():
        @pl.loop(0, chunks)
        def _(k):
            section_copy(k).wait_send()

    for e in range(2 * TICKS):
        for d, (dr, dc) in enumerate(DIRECTIONS):
            @pl.when(exists(dr, dc))
            def _(e=e, d=d, dr=dr, dc=dc):
                if dr != 0:
                    edge_copy(e, d).wait_send()
                else:
                    @pl.loop(0, chunks)
                    def _(k):
                        col_copy(e, (dc + 1) // 2, k).wait_send()


def per_device(sizes, state, fresh, conv_first, conv_second, gains, shifts):
    height, width, chan = fresh.shape
    chunks = height // CHUNK
    first = conv_first[0].reshape(3, 3 * chan, chan)
    second = conv_second[0].reshape(3, 3 * chan, chan)
    steps = 2 * TICKS
    tile = pltpu.VMEM((height, width, chan), jnp.bfloat16)
    weight = pltpu.VMEM((3, 3 * chan, chan), jnp.bfloat16)
    stack = pltpu.VMEM((height + 2, width, 3 * chan), jnp.bfloat16)
    scale = pltpu.VMEM(gains.shape[1:], jnp.float32)
    anywhere = pl.BlockSpec(memory_space=pl.ANY)
    result = pl.pallas_call(
        functools.partial(kernel, *sizes),
        out_shape=jax.ShapeDtypeStruct((TICKS, height, width, chan), jnp.bfloat16),
        in_specs=[anywhere] * 6,
        out_specs=anywhere,
        scratch_shapes=[
            scale, scale, tile, tile, tile, tile, weight, weight, stack, stack,
            pltpu.VMEM((steps, 2, width, chan), jnp.bfloat16),
            pltpu.VMEM((steps, 2, height, chan), jnp.float32),
            pltpu.VMEM((steps, 2, width, chan), jnp.bfloat16),
            pltpu.VMEM((steps, 2, height, chan), jnp.float32),
            pltpu.VMEM((steps, 2, 2, 8, chan), jnp.float32),
            pltpu.SemaphoreType.DMA((6,)),
            pltpu.SemaphoreType.DMA((TICKS, chunks)),
            pltpu.SemaphoreType.DMA((steps, 8)),
            pltpu.SemaphoreType.DMA((steps, 8)),
            pltpu.SemaphoreType.DMA((steps, 2, chunks)),
            pltpu.SemaphoreType.DMA((steps, 2, chunks)),
            pltpu.SemaphoreType.DMA((chunks,)),
            pltpu.SemaphoreType.DMA((chunks,)),
        ],
        compiler_params=pltpu.CompilerParams(
            collective_id=0, has_side_effects=True, vmem_limit_bytes=62 * 1024 * 1024
        ),
    )(state[0], fresh, first, second, gains[0], shifts[0])
    return result[:, None]


def solution(mesh):
    sizes = tuple(mesh.shape[axis] for axis in ("section", "row", "col"))
    in_specs = (
        P("section", "row", "col", None),
        P("row", "col", None),
        P("section", None, None, None, None),
        P("section", None, None, None, None),
        P("section", None, None),
        P("section", None, None),
    )
    out_specs = P(None, "section", "row", "col", None)
    return jax.shard_map(
        functools.partial(per_device, sizes),
        mesh=mesh, in_specs=in_specs, out_specs=out_specs, check_vma=False,
    )
```

```python
import functools

import jax
import jax.numpy as jnp
from jax import lax
from jax.experimental import pallas as pl
from jax.experimental.pallas import tpu as pltpu
from jax.sharding import PartitionSpec as P

TICKS = 2
CHUNK = 8
DIRECTIONS = ((-1, 0), (1, 0), (0, -1), (0, 1), (-1, -1), (-1, 1), (1, -1), (1, 1))
MESH = pl.DeviceIdType.MESH


def kernel(
    sections, rows_n, cols_n,
    state, fresh, first, second, gains_in, shifts_in, out,
    gains, shifts, x0, x1, out0, out1, w1, w2, stk_x, stk_h,
    out_row, out_col, halo_row, halo_col, halo_cor,
    in_sem, out_sem, send_sem, recv_sem, col_send, col_recv, sec_send, sec_recv,
):
    height, width, chan = x0.shape
    chunks = height // CHUNK
    sec = lax.axis_index("section")
    row = lax.axis_index("row")
    col = lax.axis_index("col")

    def when(condition):
        if isinstance(condition, bool):
            return lambda f: f() if condition else None
        return pl.when(condition)

    def start_of(k):
        return k * CHUNK if isinstance(k, int) else pl.multiple_of(k * CHUNK, CHUNK)

    def exists(dr, dc):
        return (row + dr >= 0) & (row + dr < rows_n) & (col + dc >= 0) & (col + dc < cols_n)

    def target(dr, dc):
        return {"row": row + dr, "col": col + dc}

    copies = [
        pltpu.make_async_copy(src, dst, in_sem.at[n])
        for n, (src, dst) in enumerate(
            ((state, x0), (first, w1), (gains_in, gains), (shifts_in, shifts), (second, w2))
        )
    ]
    fresh_copy = pltpu.make_async_copy(fresh, x1, in_sem.at[5])
    for copy in copies:
        copy.start()

    @pl.when(sec == 0)
    def _():
        fresh_copy.start()

    halo_row[...] = jnp.zeros_like(halo_row)
    halo_col[...] = jnp.zeros_like(halo_col)
    halo_cor[...] = jnp.zeros_like(halo_cor)

    barrier = pltpu.get_barrier_semaphore()
    count = jnp.int32(0)
    for dr, dc in DIRECTIONS:
        there = exists(dr, dc)
        count = count + there.astype(jnp.int32)

        @pl.when(there)
        def _(dr=dr, dc=dc):
            pl.semaphore_signal(barrier, inc=1, device_id=target(dr, dc), device_id_type=MESH)

    for ds in (-1, 1):
        there = (sec + ds >= 0) & (sec + ds < sections)
        count = count + there.astype(jnp.int32)

        @pl.when(there)
        def _(ds=ds):
            pl.semaphore_signal(barrier, inc=1, device_id={"section": sec + ds}, device_id_type=MESH)

    def edge_copy(e, d):
        dr, dc = DIRECTIONS[d]
        if dc == 0:
            src, dst = out_row.at[e, (dr + 1) // 2], halo_row.at[e, (1 - dr) // 2]
        else:
            start = 0 if dr < 0 else height - 8
            src = out_col.at[e, (dc + 1) // 2, pl.ds(start, 8)]
            dst = halo_cor.at[e, (1 - dr) // 2, (1 - dc) // 2]
        return pltpu.make_async_remote_copy(
            src_ref=src, dst_ref=dst, send_sem=send_sem.at[e, d], recv_sem=recv_sem.at[e, d],
            device_id=target(dr, dc), device_id_type=MESH,
        )

    def col_copy(e, side, k):
        rows = pl.ds(start_of(k), CHUNK)
        return pltpu.make_async_remote_copy(
            src_ref=out_col.at[e, side, rows], dst_ref=halo_col.at[e, 1 - side, rows],
            send_sem=col_send.at[e, side, k], recv_sem=col_recv.at[e, side, k],
            device_id=target(0, 2 * side - 1), device_id_type=MESH,
        )

    def send_rows(e, way):
        for d, (dr, dc) in enumerate(DIRECTIONS):
            if dr == way:
                @pl.when(exists(dr, dc))
                def _(d=d):
                    edge_copy(e, d).start()

    def send(e, k):
        for side in range(2):
            @pl.when(exists(0, 2 * side - 1))
            def _(side=side):
                col_copy(e, side, k).start()

        @when(k == 0)
        def _():
            send_rows(e, -1)

        @when(k == chunks - 1)
        def _():
            send_rows(e, 1)

    def column(shape):
        return lax.broadcasted_iota(jnp.int32, shape, 1)

    def put(stk, at, values, left, right):
        n = values.shape[0]
        at_col = column(values.shape)
        stk[pl.ds(at, n), :, chan : 2 * chan] = values.astype(jnp.bfloat16)
        stk[pl.ds(at, n), :, :chan] = jnp.where(
            at_col == 0, left, pltpu.roll(values, 1, 1)).astype(jnp.bfloat16)
        stk[pl.ds(at, n), :, 2 * chan :] = jnp.where(
            at_col == width - 1, right, pltpu.roll(values, width - 1, 1)).astype(jnp.bfloat16)

    def put_main(e, stk, start, values):
        put(stk, start + 1, values, 0.0, 0.0)
        rows = pl.ds(start_of(start // CHUNK) if isinstance(start, int) else pl.multiple_of(start, CHUNK), CHUNK)
        out_col[e, 0, rows] = values[:, 0, :]
        out_col[e, 1, rows] = values[:, width - 1, :]

    def fix_row(e, stk, side):
        for d, (dr, dc) in enumerate(DIRECTIONS):
            if dr == 1 - 2 * side:
                @pl.when(exists(-dr, -dc))
                def _(d=d):
                    edge_copy(e, d).wait_recv()
        at = 0 if side == 0 else height + 1
        line = 7 if side == 0 else 0
        put(
            stk, at, halo_row[e, side].astype(jnp.float32)[None],
            halo_cor[e, side, 0][line : line + 1][None],
            halo_cor[e, side, 1][line : line + 1][None],
        )

    def fix(e, stk, k):
        start = start_of(k)
        for side in range(2):
            @pl.when(exists(0, 2 * side - 1))
            def _(side=side):
                col_copy(e, 1 - side, k).wait_recv()
                part = pl.ds(0, 16) if side == 0 else pl.ds(width - 16, 16)
                lanes = pl.ds(2 * chan * side, chan)
                old = stk[pl.ds(start + 1, CHUNK), part, lanes].astype(jnp.float32)
                edge = halo_col[e, side, pl.ds(start, CHUNK)].reshape(CHUNK, 1, chan)
                stk[pl.ds(start + 1, CHUNK), part, lanes] = jnp.where(
                    column(old.shape) == 15 * side, edge, old).astype(jnp.bfloat16)

        @when(k == 0)
        def _():
            fix_row(e, stk, 0)

        @when(k == chunks - 1)
        def _():
            fix_row(e, stk, 1)

    def conv(stk, w, start):
        total = None
        for tap in range(3):
            part = stk[pl.ds(start + tap, CHUNK)].reshape(CHUNK * width, 3 * chan)
            dot = jnp.dot(part, w[tap], preferred_element_type=jnp.float32)
            total = dot if total is None else total + dot
        return total

    def section_copy(k):
        rows = pl.ds(k * CHUNK, CHUNK)
        return pltpu.make_async_remote_copy(
            src_ref=out0.at[rows], dst_ref=x1.at[rows],
            send_sem=sec_send.at[k], recv_sem=sec_recv.at[k],
            device_id={"section": sec + 1}, device_id_type=MESH,
        )

    def result_copy(tick, k):
        rows = pl.ds(k * CHUNK, CHUNK)
        src = out0 if tick == 0 else out1
        return pltpu.make_async_copy(src.at[rows], out.at[tick, rows], out_sem.at[tick, k])

    def load(tick, k):
        x = x0 if tick == 0 else x1
        e = 2 * tick
        put_main(e, stk_x, k * CHUNK, x[pl.ds(k * CHUNK, CHUNK)].astype(jnp.float32))

        @when(k == 0)
        def _():
            out_row[e, 0] = x[0]

        @when(k == chunks - 1)
        def _():
            out_row[e, 1] = x[height - 1]

    def first_conv(tick, k):
        e = 2 * tick + 1
        total = conv(stk_x, w1, k * CHUNK)
        hidden = jnp.maximum(gains[0:1] * total + shifts[0:1], 0.0)
        hidden = hidden.astype(jnp.bfloat16).astype(jnp.float32)
        put_main(e, stk_h, k * CHUNK, hidden.reshape(CHUNK, width, chan))

        @when(k == 0)
        def _():
            out_row[e, 0] = stk_h[1, :, chan : 2 * chan]

        @when(k == chunks - 1)
        def _():
            out_row[e, 1] = stk_h[height, :, chan : 2 * chan]

        send(e, k)

    def second_conv(tick, k):
        x = x0 if tick == 0 else x1
        total = gains[1:2] * conv(stk_h, w2, k * CHUNK) + shifts[1:2]
        rows = pl.ds(k * CHUNK, CHUNK)
        summed = x[rows].astype(jnp.float32) + total.reshape(CHUNK, width, chan)
        result = out0 if tick == 0 else out1
        result[rows] = jnp.maximum(summed, 0.0).astype(jnp.bfloat16)
        if tick == 0:
            @pl.when(sec + 1 < sections)
            def _():
                section_copy(k).start()
        result_copy(tick, k).start()

    copies[0].wait()

    @pl.loop(0, chunks)
    def _(k):
        load(0, k)

    pl.semaphore_wait(barrier, count)

    @pl.loop(0, chunks)
    def _(k):
        send(0, k)

    for copy in copies[1:]:
        copy.wait()

    last = chunks - 1
    order = [0, last] + list(range(1, last))
    for tick in range(TICKS):
        fixed, done = set(), set()

        def ready(k):
            return all(n in done for n in (k - 1, k, k + 1) if 0 <= n < chunks)

        def need(e, stk, k):
            for n in (k - 1, k, k + 1):
                if 0 <= n < chunks and (e, n) not in fixed:
                    fixed.add((e, n))
                    fix(e, stk, n)

        todo = list(order)
        if tick == 0:
            done.update(order)
        else:
            @pl.when(sec == 0)
            def _():
                fresh_copy.wait()

            for k in order:
                if k == order[-1] and ready(0):
                    need(2, stk_x, 0)
                    first_conv(tick, 0)
                    todo.remove(0)

                @pl.when(sec > 0)
                def _(k=k):
                    section_copy(k).wait_recv()
                load(tick, k)
                send(2, k)
                done.add(k)
        for k in todo:
            need(2 * tick, stk_x, k)
            first_conv(tick, k)
        for k in order:
            need(2 * tick + 1, stk_h, k)
            second_conv(tick, k)

    for tick in range(TICKS):
        @pl.loop(0, chunks)
        def _(k):
            result_copy(tick, k).wait()

    @pl.when(sec + 1 < sections)
    def _():
        @pl.loop(0, chunks)
        def _(k):
            section_copy(k).wait_send()

    for e in range(2 * TICKS):
        for d, (dr, dc) in enumerate(DIRECTIONS):
            @pl.when(exists(dr, dc))
            def _(e=e, d=d, dr=dr, dc=dc):
                if dr != 0:
                    edge_copy(e, d).wait_send()
                else:
                    @pl.loop(0, chunks)
                    def _(k):
                        col_copy(e, (dc + 1) // 2, k).wait_send()


def per_device(sizes, state, fresh, conv_first, conv_second, gains, shifts):
    height, width, chan = fresh.shape
    chunks = height // CHUNK
    first = conv_first[0].reshape(3, 3 * chan, chan)
    second = conv_second[0].reshape(3, 3 * chan, chan)
    steps = 2 * TICKS
    tile = pltpu.VMEM((height, width, chan), jnp.bfloat16)
    weight = pltpu.VMEM((3, 3 * chan, chan), jnp.bfloat16)
    stack = pltpu.VMEM((height + 2, width, 3 * chan), jnp.bfloat16)
    scale = pltpu.VMEM(gains.shape[1:], jnp.float32)
    anywhere = pl.BlockSpec(memory_space=pl.ANY)
    result = pl.pallas_call(
        functools.partial(kernel, *sizes),
        out_shape=jax.ShapeDtypeStruct((TICKS, height, width, chan), jnp.bfloat16),
        in_specs=[anywhere] * 6,
        out_specs=anywhere,
        scratch_shapes=[
            scale, scale, tile, tile, tile, tile, weight, weight, stack, stack,
            pltpu.VMEM((steps, 2, width, chan), jnp.bfloat16),
            pltpu.VMEM((steps, 2, height, chan), jnp.float32),
            pltpu.VMEM((steps, 2, width, chan), jnp.bfloat16),
            pltpu.VMEM((steps, 2, height, chan), jnp.float32),
            pltpu.VMEM((steps, 2, 2, 8, chan), jnp.float32),
            pltpu.SemaphoreType.DMA((6,)),
            pltpu.SemaphoreType.DMA((TICKS, chunks)),
            pltpu.SemaphoreType.DMA((steps, 8)),
            pltpu.SemaphoreType.DMA((steps, 8)),
            pltpu.SemaphoreType.DMA((steps, 2, chunks)),
            pltpu.SemaphoreType.DMA((steps, 2, chunks)),
            pltpu.SemaphoreType.DMA((chunks,)),
            pltpu.SemaphoreType.DMA((chunks,)),
        ],
        compiler_params=pltpu.CompilerParams(
            collective_id=0, has_side_effects=True, vmem_limit_bytes=62 * 1024 * 1024
        ),
    )(state[0], fresh, first, second, gains[0], shifts[0])
    return result[:, None]


def solution(mesh):
    sizes = tuple(mesh.shape[axis] for axis in ("section", "row", "col"))
    in_specs = (
        P("section", "row", "col", None),
        P("row", "col", None),
        P("section", None, None, None, None),
        P("section", None, None, None, None),
        P("section", None, None),
        P("section", None, None),
    )
    out_specs = P(None, "section", "row", "col", None)
    return jax.shard_map(
        functools.partial(per_device, sizes),
        mesh=mesh, in_specs=in_specs, out_specs=out_specs, check_vma=False,
    )
```

```python
import functools

import jax
import jax.numpy as jnp
from jax import lax
from jax.experimental import pallas as pl
from jax.experimental.pallas import tpu as pltpu
from jax.sharding import PartitionSpec as P

TICKS = 2
CHUNK = 16
DIRECTIONS = ((-1, 0), (1, 0), (0, -1), (0, 1), (-1, -1), (-1, 1), (1, -1), (1, 1))
MESH = pl.DeviceIdType.MESH


def kernel(
    sections, rows_n, cols_n,
    state, fresh, first, second, gains_in, shifts_in, out,
    gains, shifts, x0, x1, out0, out1, w1, w2, stk_x, stk_h,
    out_row, out_col, halo_row, halo_col, halo_cor,
    in_sem, out_sem, send_sem, recv_sem, col_send, col_recv, sec_send, sec_recv,
):
    height, width, chan = x0.shape
    chunks = height // CHUNK
    sec = lax.axis_index("section")
    row = lax.axis_index("row")
    col = lax.axis_index("col")

    def when(condition):
        if isinstance(condition, bool):
            return lambda f: f() if condition else None
        return pl.when(condition)

    def start_of(k):
        return k * CHUNK if isinstance(k, int) else pl.multiple_of(k * CHUNK, CHUNK)

    def exists(dr, dc):
        return (row + dr >= 0) & (row + dr < rows_n) & (col + dc >= 0) & (col + dc < cols_n)

    def target(dr, dc):
        return {"row": row + dr, "col": col + dc}

    copies = [
        pltpu.make_async_copy(src, dst, in_sem.at[n])
        for n, (src, dst) in enumerate(
            ((state, x0), (first, w1), (gains_in, gains), (shifts_in, shifts), (second, w2))
        )
    ]
    fresh_copy = pltpu.make_async_copy(fresh, x1, in_sem.at[5])
    for copy in copies:
        copy.start()

    @pl.when(sec == 0)
    def _():
        fresh_copy.start()

    halo_row[...] = jnp.zeros_like(halo_row)
    halo_col[...] = jnp.zeros_like(halo_col)
    halo_cor[...] = jnp.zeros_like(halo_cor)

    barrier = pltpu.get_barrier_semaphore()
    count = jnp.int32(0)
    for dr, dc in DIRECTIONS:
        there = exists(dr, dc)
        count = count + there.astype(jnp.int32)

        @pl.when(there)
        def _(dr=dr, dc=dc):
            pl.semaphore_signal(barrier, inc=1, device_id=target(dr, dc), device_id_type=MESH)

    for ds in (-1, 1):
        there = (sec + ds >= 0) & (sec + ds < sections)
        count = count + there.astype(jnp.int32)

        @pl.when(there)
        def _(ds=ds):
            pl.semaphore_signal(barrier, inc=1, device_id={"section": sec + ds}, device_id_type=MESH)

    def edge_copy(e, d):
        dr, dc = DIRECTIONS[d]
        if dc == 0:
            src, dst = out_row.at[e, (dr + 1) // 2], halo_row.at[e, (1 - dr) // 2]
        else:
            start = 0 if dr < 0 else height - 8
            src = out_col.at[e, (dc + 1) // 2, pl.ds(start, 8)]
            dst = halo_cor.at[e, (1 - dr) // 2, (1 - dc) // 2]
        return pltpu.make_async_remote_copy(
            src_ref=src, dst_ref=dst, send_sem=send_sem.at[e, d], recv_sem=recv_sem.at[e, d],
            device_id=target(dr, dc), device_id_type=MESH,
        )

    def col_copy(e, side, k):
        rows = pl.ds(start_of(k), CHUNK)
        return pltpu.make_async_remote_copy(
            src_ref=out_col.at[e, side, rows], dst_ref=halo_col.at[e, 1 - side, rows],
            send_sem=col_send.at[e, side, k], recv_sem=col_recv.at[e, side, k],
            device_id=target(0, 2 * side - 1), device_id_type=MESH,
        )

    def send_rows(e, way):
        for d, (dr, dc) in enumerate(DIRECTIONS):
            if dr == way:
                @pl.when(exists(dr, dc))
                def _(d=d):
                    edge_copy(e, d).start()

    def send(e, k):
        for side in range(2):
            @pl.when(exists(0, 2 * side - 1))
            def _(side=side):
                col_copy(e, side, k).start()

        @when(k == 0)
        def _():
            send_rows(e, -1)

        @when(k == chunks - 1)
        def _():
            send_rows(e, 1)

    def column(shape):
        return lax.broadcasted_iota(jnp.int32, shape, 1)

    def put(stk, at, values, left, right):
        n = values.shape[0]
        at_col = column(values.shape)
        stk[pl.ds(at, n), :, chan : 2 * chan] = values.astype(jnp.bfloat16)
        stk[pl.ds(at, n), :, :chan] = jnp.where(
            at_col == 0, left, pltpu.roll(values, 1, 1)).astype(jnp.bfloat16)
        stk[pl.ds(at, n), :, 2 * chan :] = jnp.where(
            at_col == width - 1, right, pltpu.roll(values, width - 1, 1)).astype(jnp.bfloat16)

    def put_main(e, stk, start, values):
        put(stk, start + 1, values, 0.0, 0.0)
        rows = pl.ds(start_of(start // CHUNK) if isinstance(start, int) else pl.multiple_of(start, CHUNK), CHUNK)
        out_col[e, 0, rows] = values[:, 0, :]
        out_col[e, 1, rows] = values[:, width - 1, :]

    def fix_row(e, stk, side):
        for d, (dr, dc) in enumerate(DIRECTIONS):
            if dr == 1 - 2 * side:
                @pl.when(exists(-dr, -dc))
                def _(d=d):
                    edge_copy(e, d).wait_recv()
        at = 0 if side == 0 else height + 1
        line = 7 if side == 0 else 0
        put(
            stk, at, halo_row[e, side].astype(jnp.float32)[None],
            halo_cor[e, side, 0][line : line + 1][None],
            halo_cor[e, side, 1][line : line + 1][None],
        )

    def fix(e, stk, k):
        start = start_of(k)
        for side in range(2):
            @pl.when(exists(0, 2 * side - 1))
            def _(side=side):
                col_copy(e, 1 - side, k).wait_recv()
                part = pl.ds(0, 16) if side == 0 else pl.ds(width - 16, 16)
                lanes = pl.ds(2 * chan * side, chan)
                old = stk[pl.ds(start + 1, CHUNK), part, lanes].astype(jnp.float32)
                edge = halo_col[e, side, pl.ds(start, CHUNK)].reshape(CHUNK, 1, chan)
                stk[pl.ds(start + 1, CHUNK), part, lanes] = jnp.where(
                    column(old.shape) == 15 * side, edge, old).astype(jnp.bfloat16)

        @when(k == 0)
        def _():
            fix_row(e, stk, 0)

        @when(k == chunks - 1)
        def _():
            fix_row(e, stk, 1)

    def conv(stk, w, start):
        total = None
        for tap in range(3):
            part = stk[pl.ds(start + tap, CHUNK)].reshape(CHUNK * width, 3 * chan)
            dot = jnp.dot(part, w[tap], preferred_element_type=jnp.float32)
            total = dot if total is None else total + dot
        return total

    def section_copy(k):
        rows = pl.ds(k * CHUNK, CHUNK)
        return pltpu.make_async_remote_copy(
            src_ref=out0.at[rows], dst_ref=x1.at[rows],
            send_sem=sec_send.at[k], recv_sem=sec_recv.at[k],
            device_id={"section": sec + 1}, device_id_type=MESH,
        )

    def result_copy(tick, k):
        rows = pl.ds(k * CHUNK, CHUNK)
        src = out0 if tick == 0 else out1
        return pltpu.make_async_copy(src.at[rows], out.at[tick, rows], out_sem.at[tick, k])

    def load(tick, k):
        x = x0 if tick == 0 else x1
        e = 2 * tick
        put_main(e, stk_x, k * CHUNK, x[pl.ds(k * CHUNK, CHUNK)].astype(jnp.float32))

        @when(k == 0)
        def _():
            out_row[e, 0] = x[0]

        @when(k == chunks - 1)
        def _():
            out_row[e, 1] = x[height - 1]

    def first_conv(tick, k):
        e = 2 * tick + 1
        total = conv(stk_x, w1, k * CHUNK)
        hidden = jnp.maximum(gains[0:1] * total + shifts[0:1], 0.0)
        hidden = hidden.astype(jnp.bfloat16).astype(jnp.float32)
        put_main(e, stk_h, k * CHUNK, hidden.reshape(CHUNK, width, chan))

        @when(k == 0)
        def _():
            out_row[e, 0] = stk_h[1, :, chan : 2 * chan]

        @when(k == chunks - 1)
        def _():
            out_row[e, 1] = stk_h[height, :, chan : 2 * chan]

        send(e, k)

    def second_conv(tick, k):
        x = x0 if tick == 0 else x1
        total = gains[1:2] * conv(stk_h, w2, k * CHUNK) + shifts[1:2]
        rows = pl.ds(k * CHUNK, CHUNK)
        summed = x[rows].astype(jnp.float32) + total.reshape(CHUNK, width, chan)
        result = out0 if tick == 0 else out1
        result[rows] = jnp.maximum(summed, 0.0).astype(jnp.bfloat16)
        if tick == 0:
            @pl.when(sec + 1 < sections)
            def _():
                section_copy(k).start()
        result_copy(tick, k).start()

    copies[0].wait()

    @pl.loop(0, chunks)
    def _(k):
        load(0, k)

    pl.semaphore_wait(barrier, count)

    @pl.loop(0, chunks)
    def _(k):
        send(0, k)

    for copy in copies[1:]:
        copy.wait()

    last = chunks - 1
    order = [0, last] + list(range(1, last))
    for tick in range(TICKS):
        fixed, done = set(), set()

        def ready(k):
            return all(n in done for n in (k - 1, k, k + 1) if 0 <= n < chunks)

        def need(e, stk, k):
            for n in (k - 1, k, k + 1):
                if 0 <= n < chunks and (e, n) not in fixed:
                    fixed.add((e, n))
                    fix(e, stk, n)

        todo = list(order)
        if tick == 0:
            done.update(order)
        else:
            @pl.when(sec == 0)
            def _():
                fresh_copy.wait()

            for k in order:
                if k == order[-1] and ready(0):
                    need(2, stk_x, 0)
                    first_conv(tick, 0)
                    todo.remove(0)

                @pl.when(sec > 0)
                def _(k=k):
                    section_copy(k).wait_recv()
                load(tick, k)
                send(2, k)
                done.add(k)
        for k in todo:
            need(2 * tick, stk_x, k)
            first_conv(tick, k)
        for k in order:
            need(2 * tick + 1, stk_h, k)
            second_conv(tick, k)

    for tick in range(TICKS):
        @pl.loop(0, chunks)
        def _(k):
            result_copy(tick, k).wait()

    @pl.when(sec + 1 < sections)
    def _():
        @pl.loop(0, chunks)
        def _(k):
            section_copy(k).wait_send()

    for e in range(2 * TICKS):
        for d, (dr, dc) in enumerate(DIRECTIONS):
            @pl.when(exists(dr, dc))
            def _(e=e, d=d, dr=dr, dc=dc):
                if dr != 0:
                    edge_copy(e, d).wait_send()
                else:
                    @pl.loop(0, chunks)
                    def _(k):
                        col_copy(e, (dc + 1) // 2, k).wait_send()


def per_device(sizes, state, fresh, conv_first, conv_second, gains, shifts):
    height, width, chan = fresh.shape
    chunks = height // CHUNK
    first = conv_first[0].reshape(3, 3 * chan, chan)
    second = conv_second[0].reshape(3, 3 * chan, chan)
    steps = 2 * TICKS
    tile = pltpu.VMEM((height, width, chan), jnp.bfloat16)
    weight = pltpu.VMEM((3, 3 * chan, chan), jnp.bfloat16)
    stack = pltpu.VMEM((height + 2, width, 3 * chan), jnp.bfloat16)
    scale = pltpu.VMEM(gains.shape[1:], jnp.float32)
    anywhere = pl.BlockSpec(memory_space=pl.ANY)
    result = pl.pallas_call(
        functools.partial(kernel, *sizes),
        out_shape=jax.ShapeDtypeStruct((TICKS, height, width, chan), jnp.bfloat16),
        in_specs=[anywhere] * 6,
        out_specs=anywhere,
        scratch_shapes=[
            scale, scale, tile, tile, tile, tile, weight, weight, stack, stack,
            pltpu.VMEM((steps, 2, width, chan), jnp.bfloat16),
            pltpu.VMEM((steps, 2, height, chan), jnp.float32),
            pltpu.VMEM((steps, 2, width, chan), jnp.bfloat16),
            pltpu.VMEM((steps, 2, height, chan), jnp.float32),
            pltpu.VMEM((steps, 2, 2, 8, chan), jnp.float32),
            pltpu.SemaphoreType.DMA((6,)),
            pltpu.SemaphoreType.DMA((TICKS, chunks)),
            pltpu.SemaphoreType.DMA((steps, 8)),
            pltpu.SemaphoreType.DMA((steps, 8)),
            pltpu.SemaphoreType.DMA((steps, 2, chunks)),
            pltpu.SemaphoreType.DMA((steps, 2, chunks)),
            pltpu.SemaphoreType.DMA((chunks,)),
            pltpu.SemaphoreType.DMA((chunks,)),
        ],
        compiler_params=pltpu.CompilerParams(
            collective_id=0, has_side_effects=True, vmem_limit_bytes=62 * 1024 * 1024
        ),
    )(state[0], fresh, first, second, gains[0], shifts[0])
    return result[:, None]


def solution(mesh):
    sizes = tuple(mesh.shape[axis] for axis in ("section", "row", "col"))
    in_specs = (
        P("section", "row", "col", None),
        P("row", "col", None),
        P("section", None, None, None, None),
        P("section", None, None, None, None),
        P("section", None, None),
        P("section", None, None),
    )
    out_specs = P(None, "section", "row", "col", None)
    return jax.shard_map(
        functools.partial(per_device, sizes),
        mesh=mesh, in_specs=in_specs, out_specs=out_specs, check_vma=False,
    )
```

```python
import functools

import jax
import jax.numpy as jnp
from jax import lax
from jax.experimental import pallas as pl
from jax.experimental.pallas import tpu as pltpu
from jax.sharding import PartitionSpec as P

TICKS = 2
CHUNK = 8
DIRECTIONS = ((-1, 0), (1, 0), (0, -1), (0, 1), (-1, -1), (-1, 1), (1, -1), (1, 1))
MESH = pl.DeviceIdType.MESH


def kernel(
    sections, rows_n, cols_n,
    state, fresh, first, second, gains_in, shifts_in, out,
    gains, shifts, x0, x1, out0, out1, w1, w2, stk_x, stk_h,
    out_row, out_col, halo_row, halo_col, halo_cor,
    in_sem, out_sem, send_sem, recv_sem, col_send, col_recv, sec_send, sec_recv,
):
    height, width, chan = x0.shape
    chunks = height // CHUNK
    sec = lax.axis_index("section")
    row = lax.axis_index("row")
    col = lax.axis_index("col")

    def when(condition):
        if isinstance(condition, bool):
            return lambda f: f() if condition else None
        return pl.when(condition)

    def start_of(k):
        return k * CHUNK if isinstance(k, int) else pl.multiple_of(k * CHUNK, CHUNK)

    def exists(dr, dc):
        return (row + dr >= 0) & (row + dr < rows_n) & (col + dc >= 0) & (col + dc < cols_n)

    def target(dr, dc):
        return {"row": row + dr, "col": col + dc}

    copies = [
        pltpu.make_async_copy(src, dst, in_sem.at[n])
        for n, (src, dst) in enumerate(
            ((state, x0), (first, w1), (gains_in, gains), (shifts_in, shifts), (second, w2))
        )
    ]
    fresh_copy = pltpu.make_async_copy(fresh, x1, in_sem.at[5])
    for copy in copies:
        copy.start()

    @pl.when(sec == 0)
    def _():
        fresh_copy.start()

    halo_row[...] = jnp.zeros_like(halo_row)
    halo_col[...] = jnp.zeros_like(halo_col)
    halo_cor[...] = jnp.zeros_like(halo_cor)

    barrier = pltpu.get_barrier_semaphore()
    count = jnp.int32(0)
    for dr, dc in DIRECTIONS:
        there = exists(dr, dc)
        count = count + there.astype(jnp.int32)

        @pl.when(there)
        def _(dr=dr, dc=dc):
            pl.semaphore_signal(barrier, inc=1, device_id=target(dr, dc), device_id_type=MESH)

    for ds in (-1, 1):
        there = (sec + ds >= 0) & (sec + ds < sections)
        count = count + there.astype(jnp.int32)

        @pl.when(there)
        def _(ds=ds):
            pl.semaphore_signal(barrier, inc=1, device_id={"section": sec + ds}, device_id_type=MESH)

    def edge_copy(e, d):
        dr, dc = DIRECTIONS[d]
        if dc == 0:
            src, dst = out_row.at[e, (dr + 1) // 2], halo_row.at[e, (1 - dr) // 2]
        else:
            start = 0 if dr < 0 else height - 8
            src = out_col.at[e, (dc + 1) // 2, pl.ds(start, 8)]
            dst = halo_cor.at[e, (1 - dr) // 2, (1 - dc) // 2]
        return pltpu.make_async_remote_copy(
            src_ref=src, dst_ref=dst, send_sem=send_sem.at[e, d], recv_sem=recv_sem.at[e, d],
            device_id=target(dr, dc), device_id_type=MESH,
        )

    def col_copy(e, side, k):
        rows = pl.ds(start_of(k), CHUNK)
        return pltpu.make_async_remote_copy(
            src_ref=out_col.at[e, side, rows], dst_ref=halo_col.at[e, 1 - side, rows],
            send_sem=col_send.at[e, side, k], recv_sem=col_recv.at[e, side, k],
            device_id=target(0, 2 * side - 1), device_id_type=MESH,
        )

    def send_rows(e, way):
        for d, (dr, dc) in enumerate(DIRECTIONS):
            if dr == way:
                @pl.when(exists(dr, dc))
                def _(d=d):
                    edge_copy(e, d).start()

    def send(e, k):
        for side in range(2):
            @pl.when(exists(0, 2 * side - 1))
            def _(side=side):
                col_copy(e, side, k).start()

        @when(k == 0)
        def _():
            send_rows(e, -1)

        @when(k == chunks - 1)
        def _():
            send_rows(e, 1)

    def column(shape):
        return lax.broadcasted_iota(jnp.int32, shape, 1)

    def put(stk, at, values, left, right):
        n = values.shape[0]
        at_col = column(values.shape)
        stk[pl.ds(at, n), :, chan : 2 * chan] = values.astype(jnp.bfloat16)
        stk[pl.ds(at, n), :, :chan] = jnp.where(
            at_col == 0, left, pltpu.roll(values, 1, 1)).astype(jnp.bfloat16)
        stk[pl.ds(at, n), :, 2 * chan :] = jnp.where(
            at_col == width - 1, right, pltpu.roll(values, width - 1, 1)).astype(jnp.bfloat16)

    def put_main(e, stk, start, values):
        put(stk, start + 1, values, 0.0, 0.0)
        rows = pl.ds(start_of(start // CHUNK) if isinstance(start, int) else pl.multiple_of(start, CHUNK), CHUNK)
        out_col[e, 0, rows] = values[:, 0, :]
        out_col[e, 1, rows] = values[:, width - 1, :]

    def fix_row(e, stk, side):
        for d, (dr, dc) in enumerate(DIRECTIONS):
            if dr == 1 - 2 * side:
                @pl.when(exists(-dr, -dc))
                def _(d=d):
                    edge_copy(e, d).wait_recv()
        at = 0 if side == 0 else height + 1
        line = 7 if side == 0 else 0
        put(
            stk, at, halo_row[e, side].astype(jnp.float32)[None],
            halo_cor[e, side, 0][line : line + 1][None],
            halo_cor[e, side, 1][line : line + 1][None],
        )

    def fix(e, stk, k):
        start = start_of(k)
        for side in range(2):
            @pl.when(exists(0, 2 * side - 1))
            def _(side=side):
                col_copy(e, 1 - side, k).wait_recv()
                part = pl.ds(0, 16) if side == 0 else pl.ds(width - 16, 16)
                lanes = pl.ds(2 * chan * side, chan)
                old = stk[pl.ds(start + 1, CHUNK), part, lanes].astype(jnp.float32)
                edge = halo_col[e, side, pl.ds(start, CHUNK)].reshape(CHUNK, 1, chan)
                stk[pl.ds(start + 1, CHUNK), part, lanes] = jnp.where(
                    column(old.shape) == 15 * side, edge, old).astype(jnp.bfloat16)

        @when(k == 0)
        def _():
            fix_row(e, stk, 0)

        @when(k == chunks - 1)
        def _():
            fix_row(e, stk, 1)

    def conv(stk, w, start):
        total = None
        for tap in range(3):
            part = stk[pl.ds(start + tap, CHUNK)].reshape(CHUNK * width, 3 * chan)
            dot = jnp.dot(part, w[tap], preferred_element_type=jnp.float32)
            total = dot if total is None else total + dot
        return total

    def section_copy(k):
        rows = pl.ds(k * CHUNK, CHUNK)
        return pltpu.make_async_remote_copy(
            src_ref=out0.at[rows], dst_ref=x1.at[rows],
            send_sem=sec_send.at[k], recv_sem=sec_recv.at[k],
            device_id={"section": sec + 1}, device_id_type=MESH,
        )

    def result_copy(tick, k):
        rows = pl.ds(k * CHUNK, CHUNK)
        src = out0 if tick == 0 else out1
        return pltpu.make_async_copy(src.at[rows], out.at[tick, rows], out_sem.at[tick, k])

    def load(tick, k):
        x = x0 if tick == 0 else x1
        e = 2 * tick
        put_main(e, stk_x, k * CHUNK, x[pl.ds(k * CHUNK, CHUNK)].astype(jnp.float32))

        @when(k == 0)
        def _():
            out_row[e, 0] = x[0]

        @when(k == chunks - 1)
        def _():
            out_row[e, 1] = x[height - 1]

    def first_conv(tick, k):
        e = 2 * tick + 1
        total = conv(stk_x, w1, k * CHUNK)
        hidden = jnp.maximum(gains[0:1] * total + shifts[0:1], 0.0)
        hidden = hidden.astype(jnp.bfloat16).astype(jnp.float32)
        put_main(e, stk_h, k * CHUNK, hidden.reshape(CHUNK, width, chan))

        @when(k == 0)
        def _():
            out_row[e, 0] = stk_h[1, :, chan : 2 * chan]

        @when(k == chunks - 1)
        def _():
            out_row[e, 1] = stk_h[height, :, chan : 2 * chan]

        send(e, k)

    def second_conv(tick, k):
        x = x0 if tick == 0 else x1
        total = gains[1:2] * conv(stk_h, w2, k * CHUNK) + shifts[1:2]
        rows = pl.ds(k * CHUNK, CHUNK)
        summed = x[rows].astype(jnp.float32) + total.reshape(CHUNK, width, chan)
        result = out0 if tick == 0 else out1
        result[rows] = jnp.maximum(summed, 0.0).astype(jnp.bfloat16)
        if tick == 0:
            @pl.when(sec + 1 < sections)
            def _():
                section_copy(k).start()
        result_copy(tick, k).start()

    copies[0].wait()

    @pl.loop(0, chunks)
    def _(k):
        load(0, k)

    pl.semaphore_wait(barrier, count)

    @pl.loop(0, chunks)
    def _(k):
        send(0, k)

    for copy in copies[1:4]:
        copy.wait()

    last = chunks - 1
    order = [0, last] + list(range(1, last))
    for tick in range(TICKS):
        fixed, done = set(), set()

        def ready(k):
            return all(n in done for n in (k - 1, k, k + 1) if 0 <= n < chunks)

        def need(e, stk, k):
            for n in (k - 1, k, k + 1):
                if 0 <= n < chunks and (e, n) not in fixed:
                    fixed.add((e, n))
                    fix(e, stk, n)

        todo = list(order)
        if tick == 0:
            done.update(order)
        else:
            @pl.when(sec == 0)
            def _():
                fresh_copy.wait()

            for k in order:
                if k == order[-1] and ready(0):
                    need(2, stk_x, 0)
                    first_conv(tick, 0)
                    todo.remove(0)

                @pl.when(sec > 0)
                def _(k=k):
                    section_copy(k).wait_recv()
                load(tick, k)
                send(2, k)
                done.add(k)
        early = tick == 0 and chunks > 3
        for k in todo:
            need(2 * tick, stk_x, k)
            if tick == 0 and k == order[-1]:
                copies[4].wait()
                if early:
                    need(1, stk_h, 0)
                    second_conv(0, 0)
            first_conv(tick, k)
        for k in order[1:] if early else order:
            need(2 * tick + 1, stk_h, k)
            second_conv(tick, k)

    for tick in range(TICKS):
        @pl.loop(0, chunks)
        def _(k):
            result_copy(tick, k).wait()

    @pl.when(sec + 1 < sections)
    def _():
        @pl.loop(0, chunks)
        def _(k):
            section_copy(k).wait_send()

    for e in range(2 * TICKS):
        for d, (dr, dc) in enumerate(DIRECTIONS):
            @pl.when(exists(dr, dc))
            def _(e=e, d=d, dr=dr, dc=dc):
                if dr != 0:
                    edge_copy(e, d).wait_send()
                else:
                    @pl.loop(0, chunks)
                    def _(k):
                        col_copy(e, (dc + 1) // 2, k).wait_send()


def per_device(sizes, state, fresh, conv_first, conv_second, gains, shifts):
    height, width, chan = fresh.shape
    chunks = height // CHUNK
    first = conv_first[0].reshape(3, 3 * chan, chan)
    second = conv_second[0].reshape(3, 3 * chan, chan)
    steps = 2 * TICKS
    tile = pltpu.VMEM((height, width, chan), jnp.bfloat16)
    weight = pltpu.VMEM((3, 3 * chan, chan), jnp.bfloat16)
    stack = pltpu.VMEM((height + 2, width, 3 * chan), jnp.bfloat16)
    scale = pltpu.VMEM(gains.shape[1:], jnp.float32)
    anywhere = pl.BlockSpec(memory_space=pl.ANY)
    result = pl.pallas_call(
        functools.partial(kernel, *sizes),
        out_shape=jax.ShapeDtypeStruct((TICKS, height, width, chan), jnp.bfloat16),
        in_specs=[anywhere] * 6,
        out_specs=anywhere,
        scratch_shapes=[
            scale, scale, tile, tile, tile, tile, weight, weight, stack, stack,
            pltpu.VMEM((steps, 2, width, chan), jnp.bfloat16),
            pltpu.VMEM((steps, 2, height, chan), jnp.float32),
            pltpu.VMEM((steps, 2, width, chan), jnp.bfloat16),
            pltpu.VMEM((steps, 2, height, chan), jnp.float32),
            pltpu.VMEM((steps, 2, 2, 8, chan), jnp.float32),
            pltpu.SemaphoreType.DMA((6,)),
            pltpu.SemaphoreType.DMA((TICKS, chunks)),
            pltpu.SemaphoreType.DMA((steps, 8)),
            pltpu.SemaphoreType.DMA((steps, 8)),
            pltpu.SemaphoreType.DMA((steps, 2, chunks)),
            pltpu.SemaphoreType.DMA((steps, 2, chunks)),
            pltpu.SemaphoreType.DMA((chunks,)),
            pltpu.SemaphoreType.DMA((chunks,)),
        ],
        compiler_params=pltpu.CompilerParams(
            collective_id=0, has_side_effects=True, vmem_limit_bytes=62 * 1024 * 1024
        ),
    )(state[0], fresh, first, second, gains[0], shifts[0])
    return result[:, None]


def solution(mesh):
    sizes = tuple(mesh.shape[axis] for axis in ("section", "row", "col"))
    in_specs = (
        P("section", "row", "col", None),
        P("row", "col", None),
        P("section", None, None, None, None),
        P("section", None, None, None, None),
        P("section", None, None),
        P("section", None, None),
    )
    out_specs = P(None, "section", "row", "col", None)
    return jax.shard_map(
        functools.partial(per_device, sizes),
        mesh=mesh, in_specs=in_specs, out_specs=out_specs, check_vma=False,
    )
```

```python
import functools

import jax
import jax.numpy as jnp
from jax import lax
from jax.experimental import pallas as pl
from jax.experimental.pallas import tpu as pltpu
from jax.sharding import PartitionSpec as P

TICKS = 2
CHUNK = 8
DIRECTIONS = ((-1, 0), (1, 0), (0, -1), (0, 1), (-1, -1), (-1, 1), (1, -1), (1, 1))
MESH = pl.DeviceIdType.MESH


def kernel(
    sections, rows_n, cols_n,
    state, fresh, first, second, gains_in, shifts_in, out,
    gains, shifts, x0, x1, out0, out1, w1, w2, stk_x, stk_h,
    out_row, out_col, halo_row, halo_col, halo_cor,
    in_sem, out_sem, send_sem, recv_sem, col_send, col_recv, sec_send, sec_recv,
):
    height, width, chan = x0.shape
    chunks = height // CHUNK
    sec = lax.axis_index("section")
    row = lax.axis_index("row")
    col = lax.axis_index("col")

    def when(condition):
        if isinstance(condition, bool):
            return lambda f: f() if condition else None
        return pl.when(condition)

    def start_of(k):
        return k * CHUNK if isinstance(k, int) else pl.multiple_of(k * CHUNK, CHUNK)

    def exists(dr, dc):
        return (row + dr >= 0) & (row + dr < rows_n) & (col + dc >= 0) & (col + dc < cols_n)

    def target(dr, dc):
        return {"row": row + dr, "col": col + dc}

    copies = [
        pltpu.make_async_copy(src, dst, in_sem.at[n])
        for n, (src, dst) in enumerate(
            ((state, x0), (first, w1), (gains_in, gains), (shifts_in, shifts), (second, w2))
        )
    ]
    fresh_copy = pltpu.make_async_copy(fresh, x1, in_sem.at[5])
    for copy in copies:
        copy.start()

    @pl.when(sec == 0)
    def _():
        fresh_copy.start()

    halo_row[...] = jnp.zeros_like(halo_row)
    halo_col[...] = jnp.zeros_like(halo_col)
    halo_cor[...] = jnp.zeros_like(halo_cor)

    barrier = pltpu.get_barrier_semaphore()
    count = jnp.int32(0)
    for dr, dc in DIRECTIONS:
        there = exists(dr, dc)
        count = count + there.astype(jnp.int32)

        @pl.when(there)
        def _(dr=dr, dc=dc):
            pl.semaphore_signal(barrier, inc=1, device_id=target(dr, dc), device_id_type=MESH)

    for ds in (-1, 1):
        there = (sec + ds >= 0) & (sec + ds < sections)
        count = count + there.astype(jnp.int32)

        @pl.when(there)
        def _(ds=ds):
            pl.semaphore_signal(barrier, inc=1, device_id={"section": sec + ds}, device_id_type=MESH)

    def edge_copy(e, d):
        dr, dc = DIRECTIONS[d]
        if dc == 0:
            src, dst = out_row.at[e, (dr + 1) // 2], halo_row.at[e, (1 - dr) // 2]
        else:
            start = 0 if dr < 0 else height - 8
            src = out_col.at[e, (dc + 1) // 2, pl.ds(start, 8)]
            dst = halo_cor.at[e, (1 - dr) // 2, (1 - dc) // 2]
        return pltpu.make_async_remote_copy(
            src_ref=src, dst_ref=dst, send_sem=send_sem.at[e, d], recv_sem=recv_sem.at[e, d],
            device_id=target(dr, dc), device_id_type=MESH,
        )

    def col_copy(e, side, k):
        rows = pl.ds(start_of(k), CHUNK)
        return pltpu.make_async_remote_copy(
            src_ref=out_col.at[e, side, rows], dst_ref=halo_col.at[e, 1 - side, rows],
            send_sem=col_send.at[e, side, k], recv_sem=col_recv.at[e, side, k],
            device_id=target(0, 2 * side - 1), device_id_type=MESH,
        )

    def send_rows(e, way):
        for d, (dr, dc) in enumerate(DIRECTIONS):
            if dr == way:
                @pl.when(exists(dr, dc))
                def _(d=d):
                    edge_copy(e, d).start()

    def send(e, k):
        for side in range(2):
            @pl.when(exists(0, 2 * side - 1))
            def _(side=side):
                col_copy(e, side, k).start()

        @when(k == 0)
        def _():
            send_rows(e, -1)

        @when(k == chunks - 1)
        def _():
            send_rows(e, 1)

    def column(shape):
        return lax.broadcasted_iota(jnp.int32, shape, 1)

    def put(stk, at, values, left, right):
        n = values.shape[0]
        at_col = column(values.shape)
        stk[pl.ds(at, n), :, chan : 2 * chan] = values.astype(jnp.bfloat16)
        stk[pl.ds(at, n), :, :chan] = jnp.where(
            at_col == 0, left, pltpu.roll(values, 1, 1)).astype(jnp.bfloat16)
        stk[pl.ds(at, n), :, 2 * chan :] = jnp.where(
            at_col == width - 1, right, pltpu.roll(values, width - 1, 1)).astype(jnp.bfloat16)

    def put_main(e, stk, start, values):
        put(stk, start + 1, values, 0.0, 0.0)
        rows = pl.ds(start_of(start // CHUNK) if isinstance(start, int) else pl.multiple_of(start, CHUNK), CHUNK)
        for side in range(2):
            @pl.when(exists(0, 2 * side - 1))
            def _(side=side):
                part = pl.ds(0, 16) if side == 0 else pl.ds(width - 16, 16)
                near = stk[pl.ds(start + 1, CHUNK), part, chan : 2 * chan].astype(jnp.float32)
                out_col[e, side, rows] = near[:, 15 * side, :]

    def fix_row(e, stk, side):
        for d, (dr, dc) in enumerate(DIRECTIONS):
            if dr == 1 - 2 * side:
                @pl.when(exists(-dr, -dc))
                def _(d=d):
                    edge_copy(e, d).wait_recv()
        at = 0 if side == 0 else height + 1
        line = 7 if side == 0 else 0
        put(
            stk, at, halo_row[e, side].astype(jnp.float32)[None],
            halo_cor[e, side, 0][line : line + 1][None],
            halo_cor[e, side, 1][line : line + 1][None],
        )

    def fix(e, stk, k):
        start = start_of(k)
        for side in range(2):
            @pl.when(exists(0, 2 * side - 1))
            def _(side=side):
                col_copy(e, 1 - side, k).wait_recv()
                part = pl.ds(0, 16) if side == 0 else pl.ds(width - 16, 16)
                lanes = pl.ds(2 * chan * side, chan)
                old = stk[pl.ds(start + 1, CHUNK), part, lanes].astype(jnp.float32)
                edge = halo_col[e, side, pl.ds(start, CHUNK)].reshape(CHUNK, 1, chan)
                stk[pl.ds(start + 1, CHUNK), part, lanes] = jnp.where(
                    column(old.shape) == 15 * side, edge, old).astype(jnp.bfloat16)

        @when(k == 0)
        def _():
            fix_row(e, stk, 0)

        @when(k == chunks - 1)
        def _():
            fix_row(e, stk, 1)

    def conv(stk, w, start):
        total = None
        for tap in range(3):
            part = stk[pl.ds(start + tap, CHUNK)].reshape(CHUNK * width, 3 * chan)
            dot = jnp.dot(part, w[tap], preferred_element_type=jnp.float32)
            total = dot if total is None else total + dot
        return total

    def section_copy(k):
        rows = pl.ds(k * CHUNK, CHUNK)
        return pltpu.make_async_remote_copy(
            src_ref=out0.at[rows], dst_ref=x1.at[rows],
            send_sem=sec_send.at[k], recv_sem=sec_recv.at[k],
            device_id={"section": sec + 1}, device_id_type=MESH,
        )

    def result_copy(tick, k):
        rows = pl.ds(k * CHUNK, CHUNK)
        src = out0 if tick == 0 else out1
        return pltpu.make_async_copy(src.at[rows], out.at[tick, rows], out_sem.at[tick, k])

    def load(tick, k):
        x = x0 if tick == 0 else x1
        e = 2 * tick
        put_main(e, stk_x, k * CHUNK, x[pl.ds(k * CHUNK, CHUNK)].astype(jnp.float32))

        @when(k == 0)
        def _():
            out_row[e, 0] = x[0]

        @when(k == chunks - 1)
        def _():
            out_row[e, 1] = x[height - 1]

    def first_conv(tick, k):
        e = 2 * tick + 1
        total = conv(stk_x, w1, k * CHUNK)
        hidden = jnp.maximum(gains[0:1] * total + shifts[0:1], 0.0)
        hidden = hidden.astype(jnp.bfloat16).astype(jnp.float32)
        put_main(e, stk_h, k * CHUNK, hidden.reshape(CHUNK, width, chan))

        @when(k == 0)
        def _():
            out_row[e, 0] = stk_h[1, :, chan : 2 * chan]

        @when(k == chunks - 1)
        def _():
            out_row[e, 1] = stk_h[height, :, chan : 2 * chan]

        send(e, k)

    def second_conv(tick, k):
        x = x0 if tick == 0 else x1
        total = gains[1:2] * conv(stk_h, w2, k * CHUNK) + shifts[1:2]
        rows = pl.ds(k * CHUNK, CHUNK)
        summed = x[rows].astype(jnp.float32) + total.reshape(CHUNK, width, chan)
        result = out0 if tick == 0 else out1
        result[rows] = jnp.maximum(summed, 0.0).astype(jnp.bfloat16)
        if tick == 0:
            @pl.when(sec + 1 < sections)
            def _():
                section_copy(k).start()
        result_copy(tick, k).start()

    copies[0].wait()

    @pl.loop(0, chunks)
    def _(k):
        load(0, k)

    pl.semaphore_wait(barrier, count)

    @pl.loop(0, chunks)
    def _(k):
        send(0, k)

    for copy in copies[1:]:
        copy.wait()

    last = chunks - 1
    order = [0, last] + list(range(1, last))
    for tick in range(TICKS):
        fixed, done = set(), set()

        def ready(k):
            return all(n in done for n in (k - 1, k, k + 1) if 0 <= n < chunks)

        def need(e, stk, k):
            for n in (k - 1, k, k + 1):
                if 0 <= n < chunks and (e, n) not in fixed:
                    fixed.add((e, n))
                    fix(e, stk, n)

        todo = list(order)
        if tick == 0:
            done.update(order)
        else:
            @pl.when(sec == 0)
            def _():
                fresh_copy.wait()

            for k in order:
                if k == order[-1] and ready(0):
                    need(2, stk_x, 0)
                    first_conv(tick, 0)
                    todo.remove(0)

                @pl.when(sec > 0)
                def _(k=k):
                    section_copy(k).wait_recv()
                load(tick, k)
                send(2, k)
                done.add(k)
        for k in todo:
            need(2 * tick, stk_x, k)
            first_conv(tick, k)
        for k in order:
            need(2 * tick + 1, stk_h, k)
            second_conv(tick, k)

    for tick in range(TICKS):
        @pl.loop(0, chunks)
        def _(k):
            result_copy(tick, k).wait()

    @pl.when(sec + 1 < sections)
    def _():
        @pl.loop(0, chunks)
        def _(k):
            section_copy(k).wait_send()

    for e in range(2 * TICKS):
        for d, (dr, dc) in enumerate(DIRECTIONS):
            @pl.when(exists(dr, dc))
            def _(e=e, d=d, dr=dr, dc=dc):
                if dr != 0:
                    edge_copy(e, d).wait_send()
                else:
                    @pl.loop(0, chunks)
                    def _(k):
                        col_copy(e, (dc + 1) // 2, k).wait_send()


def per_device(sizes, state, fresh, conv_first, conv_second, gains, shifts):
    height, width, chan = fresh.shape
    chunks = height // CHUNK
    first = conv_first[0].reshape(3, 3 * chan, chan)
    second = conv_second[0].reshape(3, 3 * chan, chan)
    steps = 2 * TICKS
    tile = pltpu.VMEM((height, width, chan), jnp.bfloat16)
    weight = pltpu.VMEM((3, 3 * chan, chan), jnp.bfloat16)
    stack = pltpu.VMEM((height + 2, width, 3 * chan), jnp.bfloat16)
    scale = pltpu.VMEM(gains.shape[1:], jnp.float32)
    anywhere = pl.BlockSpec(memory_space=pl.ANY)
    result = pl.pallas_call(
        functools.partial(kernel, *sizes),
        out_shape=jax.ShapeDtypeStruct((TICKS, height, width, chan), jnp.bfloat16),
        in_specs=[anywhere] * 6,
        out_specs=anywhere,
        scratch_shapes=[
            scale, scale, tile, tile, tile, tile, weight, weight, stack, stack,
            pltpu.VMEM((steps, 2, width, chan), jnp.bfloat16),
            pltpu.VMEM((steps, 2, height, chan), jnp.float32),
            pltpu.VMEM((steps, 2, width, chan), jnp.bfloat16),
            pltpu.VMEM((steps, 2, height, chan), jnp.float32),
            pltpu.VMEM((steps, 2, 2, 8, chan), jnp.float32),
            pltpu.SemaphoreType.DMA((6,)),
            pltpu.SemaphoreType.DMA((TICKS, chunks)),
            pltpu.SemaphoreType.DMA((steps, 8)),
            pltpu.SemaphoreType.DMA((steps, 8)),
            pltpu.SemaphoreType.DMA((steps, 2, chunks)),
            pltpu.SemaphoreType.DMA((steps, 2, chunks)),
            pltpu.SemaphoreType.DMA((chunks,)),
            pltpu.SemaphoreType.DMA((chunks,)),
        ],
        compiler_params=pltpu.CompilerParams(
            collective_id=0, has_side_effects=True, vmem_limit_bytes=62 * 1024 * 1024
        ),
    )(state[0], fresh, first, second, gains[0], shifts[0])
    return result[:, None]


def solution(mesh):
    sizes = tuple(mesh.shape[axis] for axis in ("section", "row", "col"))
    in_specs = (
        P("section", "row", "col", None),
        P("row", "col", None),
        P("section", None, None, None, None),
        P("section", None, None, None, None),
        P("section", None, None),
        P("section", None, None),
    )
    out_specs = P(None, "section", "row", "col", None)
    return jax.shard_map(
        functools.partial(per_device, sizes),
        mesh=mesh, in_specs=in_specs, out_specs=out_specs, check_vma=False,
    )
```
